256 devices in a mesh: batch: 8 (over y, core), proto: 32 (over x, z).
Axes of the slice: x: 4, y: 4, z: 8, core: 2. Of those that a mesh axis runs over, the one named last changes fastest.
Arguments:
- features: bfloat16 [8192, 256], P(('batch', 'proto')), may hold values from -8 to 8
- head_weight: bfloat16 [256, 65536], P('batch', 'proto'), may hold values from -0.375 to 0.375
- student_scores: bfloat16 [2, 8192, 65536], P(None, 'batch', 'proto'), may hold values from -1 to 1
Outputs:
- targets: bfloat16 [8192, 65536], P('batch', 'proto')
- row_loss: float32 [2, 8192], P(None, 'batch')
The draws below stay inside these ranges and needn't reach their ends.
All inputs are finite; a program needn't handle non-finite values.
Results may differ from the reference program's by a relative error of at most 0.0013.
Values may be sent and summed in bfloat16 or wider, within the bound.
A program may use at most 64 MiB of HBM per device.

```python
import jax
import jax.numpy as jnp
from jax import lax

BOTTLENECK = 256
PROTOS = 65536
VIEWS = 2
ITERS = 3
ROWS = 8192


def centre_table(key):
    count = max(PROTOS // 1024, 4)
    centres = jax.random.normal(jax.random.fold_in(key, 101), (count, BOTTLENECK), jnp.float32)
    return (count, centres)


def draw_features(key, part):
    count, centres = centre_table(key)
    first = jax.random.randint(jax.random.fold_in(key, 21), (ROWS,), 0, count)
    second = jax.random.randint(jax.random.fold_in(key, 22), (ROWS,), 0, count)
    label = jnp.minimum(first, second).astype(jnp.int32)
    picked = centres[label]
    strength = jax.random.uniform(jax.random.fold_in(key, 23), (ROWS, 1), jnp.float32, 0.4, 1.0)
    noise = jax.random.normal(jax.random.fold_in(key, 24), (ROWS, BOTTLENECK), jnp.float32)
    values = strength * picked + noise
    return jnp.clip(values, -8.0, 8.0).astype(jnp.bfloat16)


def draw_head_weight(key, part):
    count, centres = centre_table(key)
    block = max(PROTOS // 512, 8)
    blocks = PROTOS // block
    block_label = jax.random.randint(jax.random.fold_in(key, 31), (blocks,), 0, 2 * count)
    label = jnp.repeat(block_label, block).astype(jnp.int32)
    padded = jnp.concatenate([centres, jnp.zeros((count, BOTTLENECK), jnp.float32)], axis=0)
    picked = padded[label]
    strength = jax.random.uniform(jax.random.fold_in(key, 32), (PROTOS, 1), jnp.float32, 0.5, 0.9)
    noise = jax.random.normal(jax.random.fold_in(key, 33), (PROTOS, BOTTLENECK), jnp.float32)
    values = (strength * picked + noise) * 0.05
    return jnp.clip(jnp.transpose(values), -0.375, 0.375).astype(jnp.bfloat16)


def steps_of(stream_key, extent, cuts, low, high):
    def one(axis_at, blocks):
        steps = jax.random.uniform(jax.random.fold_in(jax.random.fold_in(stream_key, 6), axis_at), (blocks,), jnp.float32, low / len(cuts), high / len(cuts))
        return jnp.repeat(jnp.exp(steps), extent[axis_at] // blocks).reshape((-1,) + (1,) * (len(extent) - axis_at - 1))

    loudness = one(*cuts[0])
    for cut in cuts[1:]:
        loudness = loudness * one(*cut)
    return loudness


def setup_inputs(seed: int = 0) -> dict:
    key_of = jax.random.split(jax.random.key(seed), 4)
    features = draw_features(jax.random.fold_in(key_of[3], 71), 0)
    head_weight = draw_head_weight(jax.random.fold_in(key_of[3], 71), 0)
    student_scores = jnp.clip(jax.random.uniform(key_of[2], (VIEWS, ROWS, PROTOS), jnp.float32, -1.0, 1.0) * steps_of(key_of[2], (VIEWS, ROWS, PROTOS), ((1, 8), (2, 32)), -0.4, 0.0), -1.0, 1.0).astype(jnp.bfloat16)
    return {"features": features, "head_weight": head_weight, "student_scores": student_scores}


TEACHER_TEMP = 0.07
STUDENT_TEMP = 0.1

def reference(features, head_weight, student_scores):
    feat_wide = features.astype(jnp.float32)
    fnorm = jnp.sqrt(lax.optimization_barrier(jnp.sum(feat_wide * feat_wide, axis=1)) + 1e-06)
    weight_wide = head_weight.astype(jnp.float32)
    wnorm = jnp.sqrt(lax.optimization_barrier(jnp.sum(weight_wide * weight_wide, axis=0)) + 1e-06)
    raw = jnp.dot(features, head_weight, preferred_element_type=jnp.float32)
    balance = jnp.exp(raw / (fnorm[:, None] * wnorm[None, :]) / TEACHER_TEMP)
    for step in range(ITERS):
        balance = balance / lax.optimization_barrier(jnp.sum(balance, axis=0, keepdims=True))
        balance = balance / lax.optimization_barrier(jnp.sum(balance, axis=1, keepdims=True))

    def one_view(view):
        logits = view.astype(jnp.float32) / STUDENT_TEMP
        lse = jnp.log(lax.optimization_barrier(jnp.sum(jnp.exp(logits), axis=1)))
        return lse - lax.optimization_barrier(jnp.sum(balance * logits, axis=1))
    row_loss = lax.map(one_view, student_scores)
    targets = (balance * PROTOS).astype(jnp.bfloat16)
    return (targets, row_loss)
```

```python
import functools
import math

import jax
import jax.numpy as jnp
from jax import lax
from jax.experimental import pallas as pl
from jax.experimental.pallas import tpu as pltpu
from jax.sharding import PartitionSpec as P

PROTOS = 65536
ITERS = 3
TEACHER_TEMP = 0.07
STUDENT_TEMP = 0.1
LOG2E = math.log2(math.e)

MESH = pl.DeviceIdType.MESH
F32 = jnp.float32
BF16 = jnp.bfloat16
NX, NY, NZ, NC = 4, 4, 8, 2
NB, NP = NY * NC, NX * NZ
ROWS, COLS, DEPTH, VIEWS = 1024, 2048, 256, 2
RB, CB = ROWS // 128, COLS // 128
FCH, WCH = ROWS // NP, DEPTH // NB
STU_CHUNKS = 8


def ring(d, n):
    return min(d, n - d)


BATCH_PEERS = sorted(
    [(dy, dc) for dy in range(NY) for dc in range(NC) if (dy, dc) != (0, 0)],
    key=lambda d: -ring(d[0], NY),
)
PROTO_PEERS = sorted(
    [(dx, dz) for dx in range(NX) for dz in range(NZ) if (dx, dz) != (0, 0)],
    key=lambda d: -(ring(d[0], NX) + ring(d[1], NZ)),
)
Z_NEAR = (1, 7, 2, 6, 3, 5, 4)
X_NEAR = (2, 1, 3)
Y_NEAR = (2, 1, 3)


def tile_cols(piece):
    return jnp.concatenate([piece] * CB, axis=1)


def kernel(
    feat_ref, head_ref, stu_hbm,
    out, loss_ref,
    feat, head, stu, balance, r_rep, part, wide, colacc, inv_w,
    col_buf, row_buf, exp_buf, dot_buf,
    own_sem, stu_sem, f_send, fz_recv, fx_recv, w_send, wy_recv, wc_recv,
    col_send, col_recv, row_send, row_recv, loss_send, loss_recv,
):
    b, p = lax.axis_index("batch"), lax.axis_index("proto")
    y, core = lax.div(b, NC), lax.rem(b, NC)
    x, z = lax.div(p, NZ), lax.rem(p, NZ)

    def batch_at(dy, dc):
        return (lax.rem(y + dy, NY) * NC + lax.rem(core + dc, NC), p)

    def proto_at(dx, dz):
        return (b, lax.rem(x + dx, NX) * NZ + lax.rem(z + dz, NZ))

    def remote(src, dst, send, recv, device):
        copy = pltpu.make_async_remote_copy(
            src_ref=src, dst_ref=dst, send_sem=send, recv_sem=recv, device_id=device, device_id_type=MESH
        )
        copy.start()

    def await_bytes(ref, sem):
        pltpu.make_async_copy(ref, ref, sem).wait()

    def feat_rows(xx, zz):
        return feat.at[pl.ds(pl.multiple_of((xx * NZ + zz) * FCH, FCH), FCH), :]

    def head_rows(yy, cc):
        return head.at[pl.ds(pl.multiple_of((yy * NC + cc) * WCH, WCH), WCH), :]

    own_f, own_w = feat_rows(x, z), head_rows(y, core)
    own_in = [
        pltpu.make_async_copy(feat_ref, own_f, own_sem.at[0]),
        pltpu.make_async_copy(head_ref, own_w, own_sem.at[1]),
    ]
    for copy in own_in:
        copy.start()

    chunk = ROWS // STU_CHUNKS
    scores_in = [
        pltpu.make_async_copy(
            stu_hbm.at[:, pl.ds(k * chunk, chunk), :], stu.at[:, pl.ds(k * chunk, chunk), :], stu_sem.at[k]
        )
        for k in range(STU_CHUNKS)
    ]
    for copy in scores_in:
        copy.start()

    barrier = pltpu.get_barrier_semaphore()
    greeted = [batch_at(*d) for d in BATCH_PEERS]
    greeted += [proto_at(0, dz) for dz in range(1, NZ)] + [proto_at(dx, 0) for dx in range(1, NX)]
    for device in greeted:
        pl.semaphore_signal(barrier, inc=1, device_id=device, device_id_type=MESH)

    for k in range(STU_CHUNKS):
        scores_in[k].wait()

        def exp_rows(i, carry, k=k):
            for v in range(VIEWS):
                row = pl.multiple_of(k * chunk + i * 16, 16)
                e = jnp.exp2(stu[v, pl.ds(row, 16), :].astype(F32) * (LOG2E / STUDENT_TEMP))
                acc = e[:, :128]
                for c in range(1, CB):
                    acc = acc + e[:, c * 128 : (c + 1) * 128]
                wide[v, pl.ds(row, 16), :] = acc
            return carry

        lax.fori_loop(0, chunk // 16, exp_rows, 0)

    pl.semaphore_wait(barrier, len(greeted))

    for copy in own_in:
        copy.wait()
    for i, dz in enumerate(Z_NEAR):
        remote(own_f, own_f, f_send, fz_recv.at[i], proto_at(0, dz))
    for i, dy in enumerate(Y_NEAR):
        remote(own_w, own_w, w_send, wy_recv.at[i], batch_at(dy, 0))
    for i, dx in enumerate(X_NEAR):
        remote(own_f, own_f, f_send, fx_recv.at[i], proto_at(dx, 0))
    remote(own_w, own_w, w_send, wc_recv, batch_at(0, 1))
    for i, dz in enumerate(Z_NEAR):
        piece = feat_rows(x, lax.rem(z + NZ - dz, NZ))
        await_bytes(piece, fz_recv.at[i])
        for j, dx in enumerate(X_NEAR):
            remote(piece, piece, f_send, fx_recv.at[j], proto_at(dx, 0))
    for i in (1, 2, 0):
        piece = head_rows(lax.rem(y + NY - Y_NEAR[i], NY), core)
        await_bytes(piece, wy_recv.at[i])
        remote(piece, piece, w_send, wc_recv, batch_at(0, 1))
    await_bytes(head.at[pl.ds(0, NY * WCH), :], wc_recv)

    for c in range(4):
        cols = pl.ds(c * 512, 512)
        w_wide = head[:, cols].astype(F32)
        inv_w[:, cols] = 1.0 / jnp.sqrt(jnp.sum(w_wide * w_wide, axis=0, keepdims=True) + 1e-06)
    colacc[...] = jnp.zeros_like(colacc)

    def fill(block):
        first = pl.multiple_of(block * (NZ * FCH), NZ * FCH)
        f_wide = feat[pl.ds(first, 256), :].astype(F32)
        inv_f = (LOG2E / TEACHER_TEMP) / jnp.sqrt(jnp.sum(f_wide * f_wide, axis=1, keepdims=True) + 1e-06)

        def columns(c, carry):
            cols = pl.ds(pl.multiple_of(c * 256, 256), 256)
            raw = jnp.dot(feat[pl.ds(first, 256), :], head[:, cols], preferred_element_type=F32)
            e = jnp.exp2(raw * inv_f * inv_w[:, cols])
            balance[pl.ds(first, 256), cols] = e
            colacc[:, cols] += jnp.sum(e.reshape(32, 8, 256), axis=0)
            return carry

        lax.fori_loop(0, COLS // 256, columns, 0)

    fill(x)
    for j in (1, 2, 0):
        block = lax.rem(x + NX - X_NEAR[j], NX)
        await_bytes(feat.at[pl.ds(pl.multiple_of(block * 256, 256), 256), :], fx_recv.at[j])
        fill(block)

    def lane_sums(get):
        return jnp.concatenate(
            [jnp.sum(get(a).T, axis=0, keepdims=True) for a in range(RB)], axis=0
        )

    def send_rows(mine, buf_of, send, recv):
        for dx, dz in PROTO_PEERS:
            remote(mine, mine, send, recv, proto_at(dx, dz))

    def total(buf, n):
        acc = buf[0]
        for k in range(1, n):
            acc = acc + buf[k]
        return acc

    for step in range(ITERS):
        if step > 0:

            def col_rows(i, acc):
                for u in range(4):
                    row = pl.multiple_of(i * 32 + u * 8, 8)
                    acc = acc + balance[pl.ds(row, 8), :] * tile_cols(r_rep[pl.ds(row, 8), :])
                return acc

            colacc[...] = lax.fori_loop(0, ROWS // 32, col_rows, jnp.zeros((8, COLS), F32))
        sums = jnp.sum(colacc[...], axis=0, keepdims=True)
        mine = col_buf.at[step, b]
        for k in range(CB):
            mine[k : k + 1, :] = sums[:, k * 128 : (k + 1) * 128]
        for dy, dc in BATCH_PEERS:
            remote(mine, mine, col_send.at[step], col_recv.at[step], batch_at(dy, dc))
        await_bytes(col_buf.at[step, pl.ds(0, NB - 1)], col_recv.at[step])
        col_inv = 1.0 / total(col_buf.at[step], NB)
        col_wide = jnp.concatenate(
            [jnp.broadcast_to(col_inv[k : k + 1, :], (8, 128)) for k in range(CB)], axis=1
        )

        def row_rows(i, carry):
            for u in range(4):
                row = pl.multiple_of(i * 32 + u * 8, 8)
                q = balance[pl.ds(row, 8), :] * col_wide
                acc = q[:, :128]
                for c in range(1, CB):
                    acc = acc + q[:, c * 128 : (c + 1) * 128]
                part[pl.ds(row, 8), :] = acc
            return carry

        lax.fori_loop(0, ROWS // 32, row_rows, 0)
        mine = row_buf.at[step, p]
        mine[...] = lane_sums(lambda a: part[a * 128 : (a + 1) * 128, :])
        send_rows(mine, row_buf, row_send.at[step], row_recv.at[step])
        if step == 0:
            mine = exp_buf.at[p]
            for v in range(VIEWS):
                mine[v] = lane_sums(lambda a: wide[v, a * 128 : (a + 1) * 128, :])
            send_rows(mine, exp_buf, loss_send.at[0], loss_recv.at[0])
        if step == ITERS - 1:

            def dot_rows(i, carry):
                row = pl.multiple_of(i * 16, 16)
                q = balance[pl.ds(row, 16), :] * jnp.concatenate([col_wide, col_wide], axis=0)
                balance[pl.ds(row, 16), :] = q
                for v in range(VIEWS):
                    t = q * stu[v, pl.ds(row, 16), :].astype(F32)
                    acc = t[:, :128]
                    for c in range(1, CB):
                        acc = acc + t[:, c * 128 : (c + 1) * 128]
                    wide[v, pl.ds(row, 16), :] = acc
                return carry

            lax.fori_loop(0, ROWS // 16, dot_rows, 0)
            mine = dot_buf.at[p]
            for v in range(VIEWS):
                mine[v] = lane_sums(lambda a: wide[v, a * 128 : (a + 1) * 128, :])
            send_rows(mine, dot_buf, loss_send.at[1], loss_recv.at[1])
        await_bytes(row_buf.at[step, pl.ds(0, NP - 1)], row_recv.at[step])
        row_inv = 1.0 / total(row_buf.at[step], NP)
        for a in range(RB):
            r_rep[a * 128 : (a + 1) * 128, :] = jnp.broadcast_to(row_inv[a : a + 1, :], (128, 128)).T

    for a in range(RB):

        def out_rows(i, carry, a=a):
            row = pl.multiple_of(a * 128 + i * 16, 16)
            q = balance[pl.ds(row, 16), :] * tile_cols(r_rep[pl.ds(row, 16), :] * float(PROTOS))
            out[pl.ds(row, 16), :] = q.astype(BF16)
            return carry

        lax.fori_loop(0, 8, out_rows, 0)

    await_bytes(exp_buf.at[pl.ds(0, NP - 1)], loss_recv.at[0])
    await_bytes(dot_buf.at[pl.ds(0, NP - 1)], loss_recv.at[1])
    exps, dots = total(exp_buf, NP), total(dot_buf, NP)
    for v in range(VIEWS):
        row_loss = jnp.log(exps[v]) - dots[v] * row_inv * (1.0 / STUDENT_TEMP)
        for a in range(RB):
            loss_ref[v : v + 1, a * 128 : (a + 1) * 128] = row_loss[a : a + 1, :]

    await_bytes(feat.at[pl.ds(0, (NP - 1) * FCH), :], f_send)
    await_bytes(head.at[pl.ds(0, (NB - 1) * WCH), :], w_send)
    for step in range(ITERS):
        await_bytes(col_buf.at[step, pl.ds(0, NB - 1)], col_send.at[step])
        await_bytes(row_buf.at[step, pl.ds(0, NP - 1)], row_send.at[step])
    await_bytes(exp_buf.at[pl.ds(0, NP - 1)], loss_send.at[0])
    await_bytes(dot_buf.at[pl.ds(0, NP - 1)], loss_send.at[1])


def local(features, head_weight, student_scores):
    dma = pltpu.SemaphoreType.DMA
    return pl.pallas_call(
        kernel,
        out_shape=(
            jax.ShapeDtypeStruct((ROWS, COLS), BF16),
            jax.ShapeDtypeStruct((VIEWS, ROWS), F32),
        ),
        in_specs=[
            pl.BlockSpec(memory_space=pltpu.HBM),
            pl.BlockSpec(memory_space=pltpu.HBM),
            pl.BlockSpec(memory_space=pltpu.HBM),
        ],
        out_specs=(pl.BlockSpec(memory_space=pltpu.VMEM), pl.BlockSpec(memory_space=pltpu.VMEM)),
        scratch_shapes=[
            pltpu.VMEM((ROWS, DEPTH), BF16),
            pltpu.VMEM((DEPTH, COLS), BF16),
            pltpu.VMEM((VIEWS, ROWS, COLS), BF16),
            pltpu.VMEM((ROWS, COLS), F32),
            pltpu.VMEM((ROWS, 128), F32),
            pltpu.VMEM((ROWS, 128), F32),
            pltpu.VMEM((VIEWS, ROWS, 128), F32),
            pltpu.VMEM((8, COLS), F32),
            pltpu.VMEM((1, COLS), F32),
            pltpu.VMEM((ITERS, NB, CB, 128), F32),
            pltpu.VMEM((ITERS, NP, RB, 128), F32),
            pltpu.VMEM((NP, VIEWS, RB, 128), F32),
            pltpu.VMEM((NP, VIEWS, RB, 128), F32),
            dma((2,)),
            dma((STU_CHUNKS,)),
            dma,
            dma((NZ - 1,)),
            dma((NX - 1,)),
            dma,
            dma((NY - 1,)),
            dma,
            dma((ITERS,)),
            dma((ITERS,)),
            dma((ITERS,)),
            dma((ITERS,)),
            dma((2,)),
            dma((2,)),
        ],
        compiler_params=pltpu.CompilerParams(
            collective_id=0, has_side_effects=True, vmem_limit_bytes=48 * 1024 * 1024
        ),
    )(features, head_weight, student_scores)


def solution(mesh):
    return jax.shard_map(
        local,
        mesh=mesh,
        in_specs=(P(("batch", "proto"), None), P("batch", "proto"), P(None, "batch", "proto")),
        out_specs=(P("batch", "proto"), P(None, "batch")),
        check_vma=False,
    )
```

```python
import functools
import math

import jax
import jax.numpy as jnp
from jax import lax
from jax.experimental import pallas as pl
from jax.experimental.pallas import tpu as pltpu
from jax.sharding import PartitionSpec as P

PROTOS = 65536
ITERS = 3
TEACHER_TEMP = 0.07
STUDENT_TEMP = 0.1
LOG2E = math.log2(math.e)

MESH = pl.DeviceIdType.MESH
F32 = jnp.float32
BF16 = jnp.bfloat16
NX, NY, NZ, NC = 4, 4, 8, 2
NB, NP = NY * NC, NX * NZ
ROWS, COLS, DEPTH, VIEWS = 1024, 2048, 256, 2
RB, CB = ROWS // 128, COLS // 128
FCH, WCH = ROWS // NP, DEPTH // NB
STU_CHUNKS = 8
VMEM_LIMIT = 48 * 1024 * 1024


def ring(d, n):
    return min(d, n - d)


BATCH_PEERS = sorted(
    [(dy, dc) for dy in range(NY) for dc in range(NC) if (dy, dc) != (0, 0)],
    key=lambda d: -ring(d[0], NY),
)
PROTO_PEERS = sorted(
    [(dx, dz) for dx in range(NX) for dz in range(NZ) if (dx, dz) != (0, 0)],
    key=lambda d: -(ring(d[0], NX) + ring(d[1], NZ)),
)
Z_NEAR = (1, 7, 2, 6, 3, 5, 4)
X_NEAR = (2, 1, 3)
Y_NEAR = (2, 1, 3)


def tile_cols(piece):
    return jnp.concatenate([piece] * CB, axis=1)


def fold(wide):
    tiles = [wide[:, k * 128 : (k + 1) * 128] for k in range(CB)]
    while len(tiles) > 1:
        tiles = [tiles[k] + tiles[k + 1] for k in range(0, len(tiles), 2)]
    return tiles[0]


def kernel(
    feat_ref, head_ref, stu_hbm,
    out, loss_ref,
    feat, head, stu, balance, r_rep, part, wide, colacc, inv_w,
    col_buf, row_buf, exp_buf, dot_buf,
    own_sem, stu_sem, f_send, fz_recv, fx_recv, w_send, wy_recv, wc_recv,
    col_send, col_recv, row_send, row_recv, loss_send, loss_recv,
):
    b, p = lax.axis_index("batch"), lax.axis_index("proto")
    y, core = lax.div(b, NC), lax.rem(b, NC)
    x, z = lax.div(p, NZ), lax.rem(p, NZ)

    def batch_at(dy, dc):
        return (lax.rem(y + dy, NY) * NC + lax.rem(core + dc, NC), p)

    def proto_at(dx, dz):
        return (b, lax.rem(x + dx, NX) * NZ + lax.rem(z + dz, NZ))

    def remote(src, dst, send, recv, device):
        copy = pltpu.make_async_remote_copy(
            src_ref=src, dst_ref=dst, send_sem=send, recv_sem=recv, device_id=device, device_id_type=MESH
        )
        copy.start()

    def await_bytes(ref, sem):
        pltpu.make_async_copy(ref, ref, sem).wait()

    def feat_rows(xx, zz):
        return feat.at[pl.ds(pl.multiple_of((xx * NZ + zz) * FCH, FCH), FCH), :]

    def head_rows(yy, cc):
        return head.at[pl.ds(pl.multiple_of((yy * NC + cc) * WCH, WCH), WCH), :]

    own_f, own_w = feat_rows(x, z), head_rows(y, core)
    own_in = [
        pltpu.make_async_copy(feat_ref, own_f, own_sem.at[0]),
        pltpu.make_async_copy(head_ref, own_w, own_sem.at[1]),
    ]
    for copy in own_in:
        copy.start()

    chunk = ROWS // STU_CHUNKS
    scores_in = [
        pltpu.make_async_copy(
            stu_hbm.at[:, pl.ds(k * chunk, chunk), :], stu.at[:, pl.ds(k * chunk, chunk), :], stu_sem.at[k]
        )
        for k in range(STU_CHUNKS)
    ]
    for copy in scores_in:
        copy.start()

    barrier = pltpu.get_barrier_semaphore()
    greeted = [batch_at(*d) for d in BATCH_PEERS]
    greeted += [proto_at(0, dz) for dz in range(1, NZ)] + [proto_at(dx, 0) for dx in range(1, NX)]
    for device in greeted:
        pl.semaphore_signal(barrier, inc=1, device_id=device, device_id_type=MESH)

    pl.semaphore_wait(barrier, len(greeted))

    for copy in own_in:
        copy.wait()
    for i, dz in enumerate(Z_NEAR):
        remote(own_f, own_f, f_send, fz_recv.at[i], proto_at(0, dz))
    for i, dy in enumerate(Y_NEAR):
        remote(own_w, own_w, w_send, wy_recv.at[i], batch_at(dy, 0))
    for i, dx in enumerate(X_NEAR):
        remote(own_f, own_f, f_send, fx_recv.at[i], proto_at(dx, 0))
    remote(own_w, own_w, w_send, wc_recv, batch_at(0, 1))
    for i, dz in enumerate(Z_NEAR):
        piece = feat_rows(x, lax.rem(z + NZ - dz, NZ))
        await_bytes(piece, fz_recv.at[i])
        for j, dx in enumerate(X_NEAR):
            remote(piece, piece, f_send, fx_recv.at[j], proto_at(dx, 0))
    for i in (1, 2, 0):
        piece = head_rows(lax.rem(y + NY - Y_NEAR[i], NY), core)
        await_bytes(piece, wy_recv.at[i])
        remote(piece, piece, w_send, wc_recv, batch_at(0, 1))
    await_bytes(head.at[pl.ds(0, NY * WCH), :], wc_recv)

    for c in range(4):
        cols = pl.ds(c * 512, 512)
        w_wide = head[:, cols].astype(F32)
        inv_w[:, cols] = 1.0 / jnp.sqrt(jnp.sum(w_wide * w_wide, axis=0, keepdims=True) + 1e-06)
    colacc[...] = jnp.zeros_like(colacc)

    def fill(block):
        first = pl.multiple_of(block * (NZ * FCH), NZ * FCH)
        f_wide = feat[pl.ds(first, 256), :].astype(F32)
        inv_f = (LOG2E / TEACHER_TEMP) / jnp.sqrt(jnp.sum(f_wide * f_wide, axis=1, keepdims=True) + 1e-06)

        raw = jnp.dot(feat[pl.ds(first, 256), :], head[...], preferred_element_type=F32)
        e = jnp.exp2(raw * inv_f * inv_w[...])
        balance[pl.ds(first, 256), :] = e
        colacc[...] += jnp.sum(e.reshape(32, 8, COLS), axis=0)

    fill(x)
    for j in (1, 2, 0):
        block = lax.rem(x + NX - X_NEAR[j], NX)
        await_bytes(feat.at[pl.ds(pl.multiple_of(block * 256, 256), 256), :], fx_recv.at[j])
        fill(block)

    def exp_sums():
        for k in range(STU_CHUNKS):
            scores_in[k].wait()

            def exp_rows(i, carry, k=k):
                for v in range(VIEWS):
                    row = pl.multiple_of(k * chunk + i * 16, 16)
                    e = jnp.exp2(stu[v, pl.ds(row, 16), :].astype(F32) * (LOG2E / STUDENT_TEMP))
                    wide[v, pl.ds(row, 16), :] = fold(e)
                return carry

            lax.fori_loop(0, chunk // 16, exp_rows, 0)

    def lane_sums(get):
        return jnp.concatenate(
            [jnp.sum(get(a).T, axis=0, keepdims=True) for a in range(RB)], axis=0
        )

    def send_rows(mine, buf_of, send, recv):
        for dx, dz in PROTO_PEERS:
            remote(mine, mine, send, recv, proto_at(dx, dz))

    def total(buf, n):
        acc = buf[0]
        for k in range(1, n):
            acc = acc + buf[k]
        return acc

    for step in range(ITERS):
        if step > 0:

            def col_rows(i, acc):
                for u in range(16):
                    row = pl.multiple_of(i * 128 + u * 8, 8)
                    acc = acc + balance[pl.ds(row, 8), :] * tile_cols(r_rep[pl.ds(row, 8), :])
                return acc

            colacc[...] = lax.fori_loop(0, ROWS // 128, col_rows, jnp.zeros((8, COLS), F32))
        sums = jnp.sum(colacc[...], axis=0, keepdims=True)
        mine = col_buf.at[step, b]
        for k in range(CB):
            mine[k : k + 1, :] = sums[:, k * 128 : (k + 1) * 128]
        for dy, dc in BATCH_PEERS:
            remote(mine, mine, col_send.at[step], col_recv.at[step], batch_at(dy, dc))
        await_bytes(col_buf.at[step, pl.ds(0, NB - 1)], col_recv.at[step])
        col_inv = 1.0 / total(col_buf.at[step], NB)
        col_wide = jnp.concatenate(
            [jnp.broadcast_to(col_inv[k : k + 1, :], (8, 128)) for k in range(CB)], axis=1
        )

        def row_rows(i, carry):
            for u in range(16):
                row = pl.multiple_of(i * 128 + u * 8, 8)
                part[pl.ds(row, 8), :] = fold(balance[pl.ds(row, 8), :] * col_wide)
            return carry

        lax.fori_loop(0, ROWS // 128, row_rows, 0)
        mine = row_buf.at[step, p]
        mine[...] = lane_sums(lambda a: part[a * 128 : (a + 1) * 128, :])
        send_rows(mine, row_buf, row_send.at[step], row_recv.at[step])
        if step == 0:
            exp_sums()
            mine = exp_buf.at[p]
            for v in range(VIEWS):
                mine[v] = lane_sums(lambda a: wide[v, a * 128 : (a + 1) * 128, :])
            send_rows(mine, exp_buf, loss_send.at[0], loss_recv.at[0])
        if step == ITERS - 1:

            for v in range(VIEWS):

                def dot_rows(i, carry, v=v):
                    for u in range(4):
                        row = pl.multiple_of(i * 64 + u * 16, 16)
                        q = balance[pl.ds(row, 16), :]
                        if v == 0:
                            q = q * jnp.concatenate([col_wide, col_wide], axis=0)
                            balance[pl.ds(row, 16), :] = q
                        wide[v, pl.ds(row, 16), :] = fold(q * stu[v, pl.ds(row, 16), :].astype(F32))
                    return carry

                lax.fori_loop(0, ROWS // 64, dot_rows, 0)
                mine = dot_buf.at[v, p]
                mine[...] = lane_sums(lambda a: wide[v, a * 128 : (a + 1) * 128, :])
                send_rows(mine, dot_buf, loss_send.at[1 + v], loss_recv.at[1 + v])
        await_bytes(row_buf.at[step, pl.ds(0, NP - 1)], row_recv.at[step])
        row_inv = 1.0 / total(row_buf.at[step], NP)
        for a in range(RB):
            r_rep[a * 128 : (a + 1) * 128, :] = jnp.broadcast_to(row_inv[a : a + 1, :], (128, 128)).T

    def out_rows(i, carry):
        for u in range(4):
            row = pl.multiple_of(i * 64 + u * 16, 16)
            q = balance[pl.ds(row, 16), :] * tile_cols(r_rep[pl.ds(row, 16), :] * float(PROTOS))
            out[pl.ds(row, 16), :] = q.astype(BF16)
        return carry

    lax.fori_loop(0, ROWS // 64, out_rows, 0)

    await_bytes(exp_buf.at[pl.ds(0, NP - 1)], loss_recv.at[0])
    for v in range(VIEWS):
        await_bytes(dot_buf.at[v, pl.ds(0, NP - 1)], loss_recv.at[1 + v])
    exps = total(exp_buf, NP)
    for v in range(VIEWS):
        row_loss = jnp.log(exps[v]) - total(dot_buf.at[v], NP) * row_inv * (1.0 / STUDENT_TEMP)
        loss_ref[v] = row_loss

    await_bytes(feat.at[pl.ds(0, (NP - 1) * FCH), :], f_send)
    await_bytes(head.at[pl.ds(0, (NB - 1) * WCH), :], w_send)
    for step in range(ITERS):
        await_bytes(col_buf.at[step, pl.ds(0, NB - 1)], col_send.at[step])
        await_bytes(row_buf.at[step, pl.ds(0, NP - 1)], row_send.at[step])
    await_bytes(exp_buf.at[pl.ds(0, NP - 1)], loss_send.at[0])
    for v in range(VIEWS):
        await_bytes(dot_buf.at[v, pl.ds(0, NP - 1)], loss_send.at[1 + v])


def finish(out, loss_in, tgt_hbm, loss_hbm, loss, sem, loss_sem):
    copies = []
    for a in range(RB):
        rows = pl.ds(a * 128, 128)
        copies.append(pltpu.make_async_copy(out.at[rows, :], tgt_hbm.at[rows, :], sem.at[a]))
        copies[-1].start()
    for v in range(VIEWS):
        for a in range(RB):
            loss[v : v + 1, a * 128 : (a + 1) * 128] = loss_in[v, a : a + 1, :]
    copies.append(pltpu.make_async_copy(loss, loss_hbm, loss_sem))
    copies[-1].start()
    for copy in copies:
        copy.wait()


def local(features, head_weight, student_scores):
    in_vmem, in_hbm = pl.BlockSpec(memory_space=pltpu.VMEM), pl.BlockSpec(memory_space=pltpu.HBM)
    dma = pltpu.SemaphoreType.DMA
    out, loss = pl.pallas_call(
        kernel,
        out_shape=(
            jax.ShapeDtypeStruct((ROWS, COLS), BF16),
            jax.ShapeDtypeStruct((VIEWS, RB, 128), F32),
        ),
        in_specs=[in_hbm] * 3,
        out_specs=(in_vmem,) * 2,
        scratch_shapes=[
            pltpu.VMEM((ROWS, DEPTH), BF16),
            pltpu.VMEM((DEPTH, COLS), BF16),
            pltpu.VMEM((VIEWS, ROWS, COLS), BF16),
            pltpu.VMEM((ROWS, COLS), F32),
            pltpu.VMEM((ROWS, 128), F32),
            pltpu.VMEM((ROWS, 128), F32),
            pltpu.VMEM((VIEWS, ROWS, 128), F32),
            pltpu.VMEM((8, COLS), F32),
            pltpu.VMEM((1, COLS), F32),
            pltpu.VMEM((ITERS, NB, CB, 128), F32),
            pltpu.VMEM((ITERS, NP, RB, 128), F32),
            pltpu.VMEM((NP, VIEWS, RB, 128), F32),
            pltpu.VMEM((VIEWS, NP, RB, 128), F32),
            dma((2,)),
            dma((STU_CHUNKS,)),
            dma,
            dma((NZ - 1,)),
            dma((NX - 1,)),
            dma,
            dma((NY - 1,)),
            dma,
            dma((ITERS,)),
            dma((ITERS,)),
            dma((ITERS,)),
            dma((ITERS,)),
            dma((1 + VIEWS,)),
            dma((1 + VIEWS,)),
        ],
        compiler_params=pltpu.CompilerParams(
            collective_id=0, has_side_effects=True, vmem_limit_bytes=VMEM_LIMIT
        ),
    )(*(pltpu.with_memory_space_constraint(a, pltpu.HBM) for a in (features, head_weight, student_scores)))
    return pl.pallas_call(
        finish,
        out_shape=(
            jax.ShapeDtypeStruct((ROWS, COLS), BF16),
            jax.ShapeDtypeStruct((VIEWS, ROWS), F32),
        ),
        in_specs=[in_vmem] * 2,
        out_specs=(in_hbm,) * 2,
        scratch_shapes=[
            pltpu.VMEM((VIEWS, ROWS), F32),
            dma((RB,)),
            dma,
        ],
        compiler_params=pltpu.CompilerParams(vmem_limit_bytes=16 * 1024 * 1024),
    )(out, loss)


def solution(mesh):
    return jax.shard_map(
        local,
        mesh=mesh,
        in_specs=(P(("batch", "proto"), None), P("batch", "proto"), P(None, "batch", "proto")),
        out_specs=(P("batch", "proto"), P(None, "batch")),
        check_vma=False,
    )
```

```python
import functools
import math

import jax
import jax.numpy as jnp
from jax import lax
from jax.experimental import pallas as pl
from jax.experimental.pallas import tpu as pltpu
from jax.sharding import PartitionSpec as P

PROTOS = 65536
ITERS = 3
TEACHER_TEMP = 0.07
STUDENT_TEMP = 0.1
LOG2E = math.log2(math.e)

MESH = pl.DeviceIdType.MESH
F32 = jnp.float32
BF16 = jnp.bfloat16
NX, NY, NZ, NC = 4, 4, 8, 2
NB, NP = NY * NC, NX * NZ
ROWS, COLS, DEPTH, VIEWS = 1024, 2048, 256, 2
RB, CB = ROWS // 128, COLS // 128
FCH, WCH = ROWS // NP, DEPTH // NB
STU_CHUNKS = 8
VMEM_LIMIT = 48 * 1024 * 1024


def ring(d, n):
    return min(d, n - d)


BATCH_PEERS = sorted(
    [(dy, dc) for dy in range(NY) for dc in range(NC) if (dy, dc) != (0, 0)],
    key=lambda d: -ring(d[0], NY),
)
PROTO_PEERS = sorted(
    [(dx, dz) for dx in range(NX) for dz in range(NZ) if (dx, dz) != (0, 0)],
    key=lambda d: -(ring(d[0], NX) + ring(d[1], NZ)),
)
Z_NEAR = (1, 7, 2, 6, 3, 5, 4)
X_NEAR = (2, 1, 3)
Y_NEAR = (2, 1, 3)


def tile_cols(piece):
    return jnp.concatenate([piece] * CB, axis=1)


def fold(wide):
    tiles = [wide[:, k * 128 : (k + 1) * 128] for k in range(CB)]
    while len(tiles) > 1:
        tiles = [tiles[k] + tiles[k + 1] for k in range(0, len(tiles), 2)]
    return tiles[0]


def kernel(
    feat_ref, head_ref, stu_hbm,
    out, loss_ref,
    feat, head, stu, balance, r_rep, part, wide, colacc, inv_w,
    col_buf, row_buf, exp_buf, dot_buf,
    own_sem, stu_sem, f_send, fz_recv, fx_recv, w_send, wy_recv, wc_recv,
    col_send, col_recv, row_send, row_recv, loss_send, loss_recv,
):
    b, p = lax.axis_index("batch"), lax.axis_index("proto")
    y, core = lax.div(b, NC), lax.rem(b, NC)
    x, z = lax.div(p, NZ), lax.rem(p, NZ)

    def batch_at(dy, dc):
        return (lax.rem(y + dy, NY) * NC + lax.rem(core + dc, NC), p)

    def proto_at(dx, dz):
        return (b, lax.rem(x + dx, NX) * NZ + lax.rem(z + dz, NZ))

    def remote(src, dst, send, recv, device):
        copy = pltpu.make_async_remote_copy(
            src_ref=src, dst_ref=dst, send_sem=send, recv_sem=recv, device_id=device, device_id_type=MESH
        )
        copy.start()

    def await_bytes(ref, sem):
        pltpu.make_async_copy(ref, ref, sem).wait()

    def feat_rows(xx, zz):
        return feat.at[pl.ds(pl.multiple_of((xx * NZ + zz) * FCH, FCH), FCH), :]

    def head_rows(yy, cc):
        return head.at[pl.ds(pl.multiple_of((yy * NC + cc) * WCH, WCH), WCH), :]

    own_f, own_w = feat_rows(x, z), head_rows(y, core)
    own_in = [
        pltpu.make_async_copy(feat_ref, own_f, own_sem.at[0]),
        pltpu.make_async_copy(head_ref, own_w, own_sem.at[1]),
    ]
    for copy in own_in:
        copy.start()

    chunk = ROWS // STU_CHUNKS
    scores_in = [
        pltpu.make_async_copy(
            stu_hbm.at[:, pl.ds(k * chunk, chunk), :], stu.at[:, pl.ds(k * chunk, chunk), :], stu_sem.at[k]
        )
        for k in range(STU_CHUNKS)
    ]
    barrier = pltpu.get_barrier_semaphore()
    greeted = [batch_at(*d) for d in BATCH_PEERS]
    greeted = [proto_at(0, dz) for dz in reversed(Z_NEAR)] + greeted + [proto_at(dx, 0) for dx in range(1, NX)]
    for device in greeted:
        pl.semaphore_signal(barrier, inc=1, device_id=device, device_id_type=MESH)

    pl.semaphore_wait(barrier, len(greeted))

    for copy in own_in:
        copy.wait()
    for i, dz in enumerate(Z_NEAR):
        remote(own_f, own_f, f_send, fz_recv.at[i], proto_at(0, dz))
    for i, dy in enumerate(Y_NEAR):
        remote(own_w, own_w, w_send, wy_recv.at[i], batch_at(dy, 0))
    for i, dx in enumerate(X_NEAR):
        remote(own_f, own_f, f_send, fx_recv.at[i], proto_at(dx, 0))
    remote(own_w, own_w, w_send, wc_recv, batch_at(0, 1))
    for copy in scores_in:
        copy.start()
    for i, dz in enumerate(Z_NEAR):
        piece = feat_rows(x, lax.rem(z + NZ - dz, NZ))
        await_bytes(piece, fz_recv.at[i])
        for j, dx in enumerate(X_NEAR):
            remote(piece, piece, f_send, fx_recv.at[j], proto_at(dx, 0))
    for i in (1, 2, 0):
        piece = head_rows(lax.rem(y + NY - Y_NEAR[i], NY), core)
        await_bytes(piece, wy_recv.at[i])
        remote(piece, piece, w_send, wc_recv, batch_at(0, 1))
    await_bytes(head.at[pl.ds(0, NY * WCH), :], wc_recv)

    for c in range(4):
        cols = pl.ds(c * 512, 512)
        w_wide = head[:, cols].astype(F32)
        inv_w[:, cols] = 1.0 / jnp.sqrt(jnp.sum(w_wide * w_wide, axis=0, keepdims=True) + 1e-06)
    colacc[...] = jnp.zeros_like(colacc)

    def fill(block):
        first = pl.multiple_of(block * (NZ * FCH), NZ * FCH)
        f_wide = feat[pl.ds(first, 256), :].astype(F32)
        inv_f = (LOG2E / TEACHER_TEMP) / jnp.sqrt(jnp.sum(f_wide * f_wide, axis=1, keepdims=True) + 1e-06)

        raw = jnp.dot(feat[pl.ds(first, 256), :], head[...], preferred_element_type=F32)
        e = jnp.exp2(raw * inv_f * inv_w[...])
        balance[pl.ds(first, 256), :] = e
        colacc[...] += jnp.sum(e.reshape(32, 8, COLS), axis=0)

    fill(x)
    for j in (1, 2, 0):
        block = lax.rem(x + NX - X_NEAR[j], NX)
        await_bytes(feat.at[pl.ds(pl.multiple_of(block * 256, 256), 256), :], fx_recv.at[j])
        fill(block)

    def exp_sums():
        for k in range(STU_CHUNKS):
            scores_in[k].wait()

            def exp_rows(i, carry, k=k):
                for v in range(VIEWS):
                    row = pl.multiple_of(k * chunk + i * 16, 16)
                    e = jnp.exp2(stu[v, pl.ds(row, 16), :].astype(F32) * (LOG2E / STUDENT_TEMP))
                    wide[v, pl.ds(row, 16), :] = fold(e)
                return carry

            lax.fori_loop(0, chunk // 16, exp_rows, 0)

    def lane_sums(get):
        return jnp.concatenate(
            [jnp.sum(get(a).T, axis=0, keepdims=True) for a in range(RB)], axis=0
        )

    def send_rows(mine, buf_of, send, recv):
        for dx, dz in PROTO_PEERS:
            remote(mine, mine, send, recv, proto_at(dx, dz))

    def total(buf, n):
        acc = buf[0]
        for k in range(1, n):
            acc = acc + buf[k]
        return acc

    for step in range(ITERS):
        if step > 0:

            def col_rows(i, acc):
                for u in range(16):
                    row = pl.multiple_of(i * 128 + u * 8, 8)
                    acc = acc + balance[pl.ds(row, 8), :] * tile_cols(r_rep[pl.ds(row, 8), :])
                return acc

            colacc[...] = lax.fori_loop(0, ROWS // 128, col_rows, jnp.zeros((8, COLS), F32))
        sums = jnp.sum(colacc[...], axis=0, keepdims=True)
        mine = col_buf.at[step, b]
        for k in range(CB):
            mine[k : k + 1, :] = sums[:, k * 128 : (k + 1) * 128]
        for dy, dc in BATCH_PEERS:
            remote(mine, mine, col_send.at[step], col_recv.at[step], batch_at(dy, dc))
        await_bytes(col_buf.at[step, pl.ds(0, NB - 1)], col_recv.at[step])
        col_inv = 1.0 / total(col_buf.at[step], NB)
        col_wide = jnp.concatenate(
            [jnp.broadcast_to(col_inv[k : k + 1, :], (8, 128)) for k in range(CB)], axis=1
        )

        def row_rows(i, carry):
            for u in range(16):
                row = pl.multiple_of(i * 128 + u * 8, 8)
                part[pl.ds(row, 8), :] = fold(balance[pl.ds(row, 8), :] * col_wide)
            return carry

        lax.fori_loop(0, ROWS // 128, row_rows, 0)
        mine = row_buf.at[step, p]
        own_sums = lane_sums(lambda a: part[a * 128 : (a + 1) * 128, :])
        mine[...] = own_sums
        send_rows(mine, row_buf, row_send.at[step], row_recv.at[step])
        if step == 0:
            exp_sums()
            mine = exp_buf.at[p]
            for v in range(VIEWS):
                mine[v] = lane_sums(lambda a: wide[v, a * 128 : (a + 1) * 128, :])
            send_rows(mine, exp_buf, loss_send.at[0], loss_recv.at[0])
        if step == ITERS - 1:
            await_bytes(exp_buf.at[pl.ds(0, NP - 1)], loss_recv.at[0])
            lse = jnp.log(total(exp_buf, NP))

            def dot_rows(i, carry):
                for u in range(2):
                    row = pl.multiple_of(i * 32 + u * 16, 16)
                    q = balance[pl.ds(row, 16), :] * jnp.concatenate([col_wide, col_wide], axis=0)
                    balance[pl.ds(row, 16), :] = q
                    for v in range(VIEWS):
                        wide[v, pl.ds(row, 16), :] = fold(q * stu[v, pl.ds(row, 16), :].astype(F32))
                return carry

            lax.fori_loop(0, ROWS // 32, dot_rows, 0)
            losses = [
                lse[v] * own_sums
                - lane_sums(lambda a: wide[v, a * 128 : (a + 1) * 128, :]) * (1.0 / STUDENT_TEMP)
                for v in range(VIEWS)
            ]
            mine = dot_buf.at[p]
            mine[...] = jnp.concatenate(losses, axis=0).astype(BF16)
            send_rows(mine, dot_buf, loss_send.at[1], loss_recv.at[1])
        await_bytes(row_buf.at[step, pl.ds(0, NP - 1)], row_recv.at[step])
        row_inv = 1.0 / total(row_buf.at[step], NP)
        for a in range(RB):
            r_rep[a * 128 : (a + 1) * 128, :] = jnp.broadcast_to(row_inv[a : a + 1, :], (128, 128)).T

    def out_rows(i, carry):
        for u in range(4):
            row = pl.multiple_of(i * 64 + u * 16, 16)
            q = balance[pl.ds(row, 16), :] * tile_cols(r_rep[pl.ds(row, 16), :] * float(PROTOS))
            out[pl.ds(row, 16), :] = q.astype(BF16)
        return carry

    lax.fori_loop(0, ROWS // 64, out_rows, 0)

    await_bytes(dot_buf.at[pl.ds(0, NP - 1)], loss_recv.at[1])
    losses = dot_buf[0].astype(F32)
    for k in range(1, NP):
        losses = losses + dot_buf[k].astype(F32)
    for v in range(VIEWS):
        loss_ref[v] = losses[v * RB : (v + 1) * RB, :] * row_inv

    await_bytes(feat.at[pl.ds(0, (NP - 1) * FCH), :], f_send)
    await_bytes(head.at[pl.ds(0, (NB - 1) * WCH), :], w_send)
    for step in range(ITERS):
        await_bytes(col_buf.at[step, pl.ds(0, NB - 1)], col_send.at[step])
        await_bytes(row_buf.at[step, pl.ds(0, NP - 1)], row_send.at[step])
    await_bytes(exp_buf.at[pl.ds(0, NP - 1)], loss_send.at[0])
    await_bytes(dot_buf.at[pl.ds(0, NP - 1)], loss_send.at[1])


def finish(out, loss_in, tgt_hbm, loss_hbm, loss, sem, loss_sem):
    copies = []
    for a in range(RB):
        rows = pl.ds(a * 128, 128)
        copies.append(pltpu.make_async_copy(out.at[rows, :], tgt_hbm.at[rows, :], sem.at[a]))
        copies[-1].start()
    for v in range(VIEWS):
        for a in range(RB):
            loss[v : v + 1, a * 128 : (a + 1) * 128] = loss_in[v, a : a + 1, :]
    copies.append(pltpu.make_async_copy(loss, loss_hbm, loss_sem))
    copies[-1].start()
    for copy in copies:
        copy.wait()


def local(features, head_weight, student_scores):
    in_vmem, in_hbm = pl.BlockSpec(memory_space=pltpu.VMEM), pl.BlockSpec(memory_space=pltpu.HBM)
    dma = pltpu.SemaphoreType.DMA
    out, loss = pl.pallas_call(
        kernel,
        out_shape=(
            jax.ShapeDtypeStruct((ROWS, COLS), BF16),
            jax.ShapeDtypeStruct((VIEWS, RB, 128), F32),
        ),
        in_specs=[in_hbm] * 3,
        out_specs=(in_vmem,) * 2,
        scratch_shapes=[
            pltpu.VMEM((ROWS, DEPTH), BF16),
            pltpu.VMEM((DEPTH, COLS), BF16),
            pltpu.VMEM((VIEWS, ROWS, COLS), BF16),
            pltpu.VMEM((ROWS, COLS), F32),
            pltpu.VMEM((ROWS, 128), F32),
            pltpu.VMEM((ROWS, 128), F32),
            pltpu.VMEM((VIEWS, ROWS, 128), F32),
            pltpu.VMEM((8, COLS), F32),
            pltpu.VMEM((1, COLS), F32),
            pltpu.VMEM((ITERS, NB, CB, 128), F32),
            pltpu.VMEM((ITERS, NP, RB, 128), F32),
            pltpu.VMEM((NP, VIEWS, RB, 128), F32),
            pltpu.VMEM((NP, VIEWS * RB, 128), BF16),
            dma((2,)),
            dma((STU_CHUNKS,)),
            dma,
            dma((NZ - 1,)),
            dma((NX - 1,)),
            dma,
            dma((NY - 1,)),
            dma,
            dma((ITERS,)),
            dma((ITERS,)),
            dma((ITERS,)),
            dma((ITERS,)),
            dma((2,)),
            dma((2,)),
        ],
        compiler_params=pltpu.CompilerParams(
            collective_id=0, has_side_effects=True, vmem_limit_bytes=VMEM_LIMIT
        ),
    )(*(pltpu.with_memory_space_constraint(a, pltpu.HBM) for a in (features, head_weight, student_scores)))
    return pl.pallas_call(
        finish,
        out_shape=(
            jax.ShapeDtypeStruct((ROWS, COLS), BF16),
            jax.ShapeDtypeStruct((VIEWS, ROWS), F32),
        ),
        in_specs=[in_vmem] * 2,
        out_specs=(in_hbm,) * 2,
        scratch_shapes=[
            pltpu.VMEM((VIEWS, ROWS), F32),
            dma((RB,)),
            dma,
        ],
        compiler_params=pltpu.CompilerParams(vmem_limit_bytes=16 * 1024 * 1024),
    )(out, loss)


def solution(mesh):
    return jax.shard_map(
        local,
        mesh=mesh,
        in_specs=(P(("batch", "proto"), None), P("batch", "proto"), P(None, "batch", "proto")),
        out_specs=(P("batch", "proto"), P(None, "batch")),
        check_vma=False,
    )
```

```python
import functools
import math

import jax
import jax.numpy as jnp
from jax import lax
from jax.experimental import pallas as pl
from jax.experimental.pallas import tpu as pltpu
from jax.sharding import PartitionSpec as P

PROTOS = 65536
ITERS = 3
TEACHER_TEMP = 0.07
STUDENT_TEMP = 0.1
LOG2E = math.log2(math.e)

MESH = pl.DeviceIdType.MESH
F32 = jnp.float32
BF16 = jnp.bfloat16
NX, NY, NZ, NC = 4, 4, 8, 2
NB, NP = NY * NC, NX * NZ
ROWS, COLS, DEPTH, VIEWS = 1024, 2048, 256, 2
RB, CB = ROWS // 128, COLS // 128
FCH, WCH = ROWS // NP, DEPTH // NB
STU_CHUNKS = 8
VMEM_LIMIT = 48 * 1024 * 1024


def ring(d, n):
    return min(d, n - d)


BATCH_PEERS = sorted(
    [(dy, dc) for dy in range(NY) for dc in range(NC) if (dy, dc) != (0, 0)],
    key=lambda d: -ring(d[0], NY),
)
PROTO_PEERS = sorted(
    [(dx, dz) for dx in range(NX) for dz in range(NZ) if (dx, dz) != (0, 0)],
    key=lambda d: -(ring(d[0], NX) + ring(d[1], NZ)),
)
Z_NEAR = (1, 7, 2, 6, 3, 5, 4)
X_NEAR = (2, 1, 3)
Y_NEAR = (2, 1, 3)


def tile_cols(piece):
    return jnp.concatenate([piece] * CB, axis=1)


def fold(wide):
    tiles = [wide[:, k * 128 : (k + 1) * 128] for k in range(CB)]
    while len(tiles) > 1:
        tiles = [tiles[k] + tiles[k + 1] for k in range(0, len(tiles), 2)]
    return tiles[0]


def kernel(
    feat_ref, head_ref, stu_hbm,
    out, loss_ref,
    feat, head, stu, balance, r_rep, part, wide, colacc, inv_w,
    col_buf, row_buf, last_buf, exp_buf, dot_buf,
    own_sem, stu_sem, f_send, fz_recv, fx_recv, w_send, wy_recv, wc_recv,
    col_send, col_recv, row_send, row_recv, loss_send, loss_recv,
):
    b, p = lax.axis_index("batch"), lax.axis_index("proto")
    y, core = lax.div(b, NC), lax.rem(b, NC)
    x, z = lax.div(p, NZ), lax.rem(p, NZ)

    def batch_at(dy, dc):
        return (lax.rem(y + dy, NY) * NC + lax.rem(core + dc, NC), p)

    def proto_at(dx, dz):
        return (b, lax.rem(x + dx, NX) * NZ + lax.rem(z + dz, NZ))

    def remote(src, dst, send, recv, device):
        copy = pltpu.make_async_remote_copy(
            src_ref=src, dst_ref=dst, send_sem=send, recv_sem=recv, device_id=device, device_id_type=MESH
        )
        copy.start()

    def await_bytes(ref, sem):
        pltpu.make_async_copy(ref, ref, sem).wait()

    def feat_rows(xx, zz):
        return feat.at[pl.ds(pl.multiple_of((xx * NZ + zz) * FCH, FCH), FCH), :]

    def head_rows(yy, cc):
        return head.at[pl.ds(pl.multiple_of((yy * NC + cc) * WCH, WCH), WCH), :]

    own_f, own_w = feat_rows(x, z), head_rows(y, core)
    own_in = [
        pltpu.make_async_copy(feat_ref, own_f, own_sem.at[0]),
        pltpu.make_async_copy(head_ref, own_w, own_sem.at[1]),
    ]
    for copy in own_in:
        copy.start()

    chunk = ROWS // STU_CHUNKS
    scores_in = [
        pltpu.make_async_copy(
            stu_hbm.at[:, pl.ds(k * chunk, chunk), :], stu.at[:, pl.ds(k * chunk, chunk), :], stu_sem.at[k]
        )
        for k in range(STU_CHUNKS)
    ]
    barrier = pltpu.get_barrier_semaphore()
    greeted = [batch_at(*d) for d in BATCH_PEERS]
    greeted = [proto_at(0, dz) for dz in reversed(Z_NEAR)] + greeted + [proto_at(dx, 0) for dx in range(1, NX)]
    for device in greeted:
        pl.semaphore_signal(barrier, inc=1, device_id=device, device_id_type=MESH)

    pl.semaphore_wait(barrier, len(greeted))

    for copy in own_in:
        copy.wait()
    for i, dz in enumerate(Z_NEAR):
        remote(own_f, own_f, f_send, fz_recv.at[i], proto_at(0, dz))
    for i, dy in enumerate(Y_NEAR):
        remote(own_w, own_w, w_send, wy_recv.at[i], batch_at(dy, 0))
    for i, dx in enumerate(X_NEAR):
        remote(own_f, own_f, f_send, fx_recv.at[i], proto_at(dx, 0))
    remote(own_w, own_w, w_send, wc_recv, batch_at(0, 1))
    for copy in scores_in:
        copy.start()
    for i, dz in enumerate(Z_NEAR):
        piece = feat_rows(x, lax.rem(z + NZ - dz, NZ))
        await_bytes(piece, fz_recv.at[i])
        for j, dx in enumerate(X_NEAR):
            remote(piece, piece, f_send, fx_recv.at[j], proto_at(dx, 0))
    for i in (1, 2, 0):
        piece = head_rows(lax.rem(y + NY - Y_NEAR[i], NY), core)
        await_bytes(piece, wy_recv.at[i])
        remote(piece, piece, w_send, wc_recv, batch_at(0, 1))
    await_bytes(head.at[pl.ds(0, NY * WCH), :], wc_recv)

    for c in range(4):
        cols = pl.ds(c * 512, 512)
        w_wide = head[:, cols].astype(F32)
        inv_w[:, cols] = 1.0 / jnp.sqrt(jnp.sum(w_wide * w_wide, axis=0, keepdims=True) + 1e-06)
    colacc[...] = jnp.zeros_like(colacc)

    def fill(block):
        first = pl.multiple_of(block * (NZ * FCH), NZ * FCH)
        f_wide = feat[pl.ds(first, 256), :].astype(F32)
        inv_f = (LOG2E / TEACHER_TEMP) / jnp.sqrt(jnp.sum(f_wide * f_wide, axis=1, keepdims=True) + 1e-06)

        raw = jnp.dot(feat[pl.ds(first, 256), :], head[...], preferred_element_type=F32)
        e = jnp.exp2(raw * inv_f * inv_w[...])
        balance[pl.ds(first, 256), :] = e
        colacc[...] += jnp.sum(e.reshape(32, 8, COLS), axis=0)

    fill(x)
    for j in (1, 2, 0):
        block = lax.rem(x + NX - X_NEAR[j], NX)
        await_bytes(feat.at[pl.ds(pl.multiple_of(block * 256, 256), 256), :], fx_recv.at[j])
        fill(block)

    def exp_sums():
        for k in range(STU_CHUNKS):
            scores_in[k].wait()

            def exp_rows(i, carry, k=k):
                for v in range(VIEWS):
                    row = pl.multiple_of(k * chunk + i * 16, 16)
                    e = jnp.exp2(stu[v, pl.ds(row, 16), :].astype(F32) * (LOG2E / STUDENT_TEMP))
                    wide[v, pl.ds(row, 16), :] = fold(e)
                return carry

            lax.fori_loop(0, chunk // 16, exp_rows, 0)

    def lane_sums(get):
        return jnp.concatenate(
            [jnp.sum(get(a).T, axis=0, keepdims=True) for a in range(RB)], axis=0
        )

    def send_rows(mine, buf_of, send, recv):
        for dx, dz in PROTO_PEERS:
            remote(mine, mine, send, recv, proto_at(dx, dz))

    def total(buf, n):
        acc = buf[0].astype(F32)
        for k in range(1, n):
            acc = acc + buf[k].astype(F32)
        return acc

    for step in range(ITERS):
        if step > 0:

            def col_rows(i, acc):
                for u in range(16):
                    row = pl.multiple_of(i * 128 + u * 8, 8)
                    acc = acc + balance[pl.ds(row, 8), :] * tile_cols(r_rep[pl.ds(row, 8), :])
                return acc

            colacc[...] = lax.fori_loop(0, ROWS // 128, col_rows, jnp.zeros((8, COLS), F32))
        sums = jnp.sum(colacc[...], axis=0, keepdims=True)
        mine = col_buf.at[step, b]
        for k in range(CB):
            mine[k : k + 1, :] = sums[:, k * 128 : (k + 1) * 128]
        for dy, dc in BATCH_PEERS:
            remote(mine, mine, col_send.at[step], col_recv.at[step], batch_at(dy, dc))
        await_bytes(col_buf.at[step, pl.ds(0, NB - 1)], col_recv.at[step])
        col_inv = 1.0 / total(col_buf.at[step], NB)
        col_wide = jnp.concatenate(
            [jnp.broadcast_to(col_inv[k : k + 1, :], (8, 128)) for k in range(CB)], axis=1
        )

        def row_rows(i, carry):
            for u in range(16):
                row = pl.multiple_of(i * 128 + u * 8, 8)
                part[pl.ds(row, 8), :] = fold(balance[pl.ds(row, 8), :] * col_wide)
            return carry

        lax.fori_loop(0, ROWS // 128, row_rows, 0)
        rows_buf = last_buf if step == ITERS - 1 else row_buf.at[step]
        mine = rows_buf.at[p]
        own_sums = lane_sums(lambda a: part[a * 128 : (a + 1) * 128, :])
        mine[...] = own_sums.astype(rows_buf.dtype)
        send_rows(mine, row_buf, row_send.at[step], row_recv.at[step])
        if step == 0:
            exp_sums()
            mine = exp_buf.at[p]
            for v in range(VIEWS):
                mine[v] = lane_sums(lambda a: wide[v, a * 128 : (a + 1) * 128, :])
            send_rows(mine, exp_buf, loss_send.at[0], loss_recv.at[0])
        if step == ITERS - 1:
            await_bytes(exp_buf.at[pl.ds(0, NP - 1)], loss_recv.at[0])
            lse = jnp.log(total(exp_buf, NP))

            def dot_rows(i, carry):
                for u in range(2):
                    row = pl.multiple_of(i * 32 + u * 16, 16)
                    q = balance[pl.ds(row, 16), :] * jnp.concatenate([col_wide, col_wide], axis=0)
                    balance[pl.ds(row, 16), :] = q
                    for v in range(VIEWS):
                        wide[v, pl.ds(row, 16), :] = fold(q * stu[v, pl.ds(row, 16), :].astype(F32))
                return carry

            lax.fori_loop(0, ROWS // 32, dot_rows, 0)
            losses = [
                lse[v] * own_sums
                - lane_sums(lambda a: wide[v, a * 128 : (a + 1) * 128, :]) * (1.0 / STUDENT_TEMP)
                for v in range(VIEWS)
            ]
            mine = dot_buf.at[p]
            mine[...] = jnp.concatenate(losses, axis=0).astype(BF16)
            send_rows(mine, dot_buf, loss_send.at[1], loss_recv.at[1])
        await_bytes(rows_buf.at[pl.ds(0, NP - 1)], row_recv.at[step])
        row_inv = 1.0 / total(rows_buf, NP)
        for a in range(RB):
            r_rep[a * 128 : (a + 1) * 128, :] = jnp.broadcast_to(row_inv[a : a + 1, :], (128, 128)).T

    def out_rows(i, carry):
        for u in range(4):
            row = pl.multiple_of(i * 64 + u * 16, 16)
            q = balance[pl.ds(row, 16), :] * tile_cols(r_rep[pl.ds(row, 16), :] * float(PROTOS))
            out[pl.ds(row, 16), :] = q.astype(BF16)
        return carry

    lax.fori_loop(0, ROWS // 64, out_rows, 0)

    await_bytes(dot_buf.at[pl.ds(0, NP - 1)], loss_recv.at[1])
    losses = dot_buf[0].astype(F32)
    for k in range(1, NP):
        losses = losses + dot_buf[k].astype(F32)
    for v in range(VIEWS):
        loss_ref[v] = losses[v * RB : (v + 1) * RB, :] * row_inv

    await_bytes(feat.at[pl.ds(0, (NP - 1) * FCH), :], f_send)
    await_bytes(head.at[pl.ds(0, (NB - 1) * WCH), :], w_send)
    for step in range(ITERS):
        await_bytes(col_buf.at[step, pl.ds(0, NB - 1)], col_send.at[step])
        rows_buf = last_buf if step == ITERS - 1 else row_buf.at[step]
        await_bytes(rows_buf.at[pl.ds(0, NP - 1)], row_send.at[step])
    await_bytes(exp_buf.at[pl.ds(0, NP - 1)], loss_send.at[0])
    await_bytes(dot_buf.at[pl.ds(0, NP - 1)], loss_send.at[1])


def finish(out, loss_in, tgt_hbm, loss_hbm, loss, sem, loss_sem):
    copies = []
    for a in range(RB):
        rows = pl.ds(a * 128, 128)
        copies.append(pltpu.make_async_copy(out.at[rows, :], tgt_hbm.at[rows, :], sem.at[a]))
        copies[-1].start()
    for v in range(VIEWS):
        for a in range(RB):
            loss[v : v + 1, a * 128 : (a + 1) * 128] = loss_in[v, a : a + 1, :]
    copies.append(pltpu.make_async_copy(loss, loss_hbm, loss_sem))
    copies[-1].start()
    for copy in copies:
        copy.wait()


def local(features, head_weight, student_scores):
    in_vmem, in_hbm = pl.BlockSpec(memory_space=pltpu.VMEM), pl.BlockSpec(memory_space=pltpu.HBM)
    dma = pltpu.SemaphoreType.DMA
    out, loss = pl.pallas_call(
        kernel,
        out_shape=(
            jax.ShapeDtypeStruct((ROWS, COLS), BF16),
            jax.ShapeDtypeStruct((VIEWS, RB, 128), F32),
        ),
        in_specs=[in_hbm] * 3,
        out_specs=(in_vmem,) * 2,
        scratch_shapes=[
            pltpu.VMEM((ROWS, DEPTH), BF16),
            pltpu.VMEM((DEPTH, COLS), BF16),
            pltpu.VMEM((VIEWS, ROWS, COLS), BF16),
            pltpu.VMEM((ROWS, COLS), F32),
            pltpu.VMEM((ROWS, 128), F32),
            pltpu.VMEM((ROWS, 128), F32),
            pltpu.VMEM((VIEWS, ROWS, 128), F32),
            pltpu.VMEM((8, COLS), F32),
            pltpu.VMEM((1, COLS), F32),
            pltpu.VMEM((ITERS, NB, CB, 128), F32),
            pltpu.VMEM((ITERS - 1, NP, RB, 128), BF16),
            pltpu.VMEM((NP, RB, 128), F32),
            pltpu.VMEM((NP, VIEWS, RB, 128), F32),
            pltpu.VMEM((NP, VIEWS * RB, 128), BF16),
            dma((2,)),
            dma((STU_CHUNKS,)),
            dma,
            dma((NZ - 1,)),
            dma((NX - 1,)),
            dma,
            dma((NY - 1,)),
            dma,
            dma((ITERS,)),
            dma((ITERS,)),
            dma((ITERS,)),
            dma((ITERS,)),
            dma((2,)),
            dma((2,)),
        ],
        compiler_params=pltpu.CompilerParams(
            collective_id=0, has_side_effects=True, vmem_limit_bytes=VMEM_LIMIT
        ),
    )(*(pltpu.with_memory_space_constraint(a, pltpu.HBM) for a in (features, head_weight, student_scores)))
    return pl.pallas_call(
        finish,
        out_shape=(
            jax.ShapeDtypeStruct((ROWS, COLS), BF16),
            jax.ShapeDtypeStruct((VIEWS, ROWS), F32),
        ),
        in_specs=[in_vmem] * 2,
        out_specs=(in_hbm,) * 2,
        scratch_shapes=[
            pltpu.VMEM((VIEWS, ROWS), F32),
            dma((RB,)),
            dma,
        ],
        compiler_params=pltpu.CompilerParams(vmem_limit_bytes=16 * 1024 * 1024),
    )(out, loss)


def solution(mesh):
    return jax.shard_map(
        local,
        mesh=mesh,
        in_specs=(P(("batch", "proto"), None), P("batch", "proto"), P(None, "batch", "proto")),
        out_specs=(P("batch", "proto"), P(None, "batch")),
        check_vma=False,
    )
```
